32 devices in a mesh: parts: 2 (over x), adapt: 16 (over z, y, core).
Axes of the slice: x: 2, y: 2, z: 4, core: 2. Of those that a mesh axis runs over, the one named last changes fastest.
Arguments:
- hidden_norm_rows: bfloat16 [256, 8192], P(('parts', 'adapt')), parts along dimension 0, may hold values from -6 to 6
- value_weight: bfloat16 [8192, 1024], P('adapt'), may hold values from -0.0625 to 0.0625
- adapter_down_weight: bfloat16 [96, 8192, 64], P('adapt'), may hold values from -0.0625 to 0.0625
- adapter_up_weight: bfloat16 [96, 64, 1024], P('adapt'), may hold values from -0.75 to 0.75
- adapter_per_block: int32 [2], P('parts'), parts along dimension 0, may hold values from 0 to 95
- block_live_rows: int32 [2], P('parts'), parts along dimension 0, may hold values from 1 to 128
- queries: bfloat16 [256, 8192], P(('parts', 'adapt')), parts along dimension 0, may hold values from -100 to 100
- incoming_key: bfloat16 [256, 1024], P(('parts', 'adapt')), parts along dimension 0, may hold values from -6 to 6
- key_cache: bfloat16 [256, 32, 1024], P(('parts', 'adapt')), parts along dimension 0, may hold values from -4 to 4
- value_cache: bfloat16 [256, 32, 1024], P(('parts', 'adapt')), parts along dimension 0, may hold values from -6 to 6
- cache_length: int32 [256], P(('parts', 'adapt')), parts along dimension 0, may hold values from 2 to 32
Outputs:
- new_value: bfloat16 [256, 1024], P(('parts', 'adapt')), parts along dimension 0
- attended: bfloat16 [256, 8192], P(('parts', 'adapt')), parts along dimension 0
The draws below stay inside these ranges and needn't reach their ends.
There are 2 independent parts, one for each index of `parts`. The reference program is written for one: setup_inputs(seed, part) draws one part's arguments, and reference() takes and returns one part's arrays. A program takes and returns all parts, laid end to end along the dimension named above; an argument that names none is the same for every part. Nothing has to cross between parts.
All inputs are finite; a program needn't handle non-finite values.
Results may differ from the reference program's by a relative error of at most 0.007.
Values may be sent and summed in bfloat16 or wider, within the bound.
A program may use at most 128 MiB of HBM per device.

```python
import jax
import jax.numpy as jnp
from jax import lax

MODEL_WIDTH = 8192
HEADS = 64
KV_HEADS = 8
HD = 128
ADAPTER_RANK = 64
BLOCK_ROWS = 128
CACHE = 32
ADAPTER_TOTAL = 96
ROWS = 128
BLOCKS = 1
KEY_VALUE_WIDTH = 1024


def draw_queries(key, part):
    key = jax.random.fold_in(key, 11)
    return jnp.clip(jax.random.normal(key, (ROWS, HEADS * HD), jnp.float32), -6.0, 6.0).astype(jnp.bfloat16)


def draw_key_cache(key, part):
    key = jax.random.fold_in(key, 12)
    return jnp.clip(jax.random.normal(key, (ROWS, CACHE, KEY_VALUE_WIDTH), jnp.float32), -4.0, 4.0).astype(jnp.bfloat16)


def draw_cache_length(key, part):
    key = jax.random.fold_in(key, 13)
    lengths = jax.random.randint(key, (ROWS,), 2, CACHE + 1, dtype=jnp.int32)
    return lengths.at[0].set(CACHE)


def draw_block_live_rows(key, part):
    key = jax.random.fold_in(key, 14)
    counts = jax.random.randint(key, (BLOCKS,), 1, BLOCK_ROWS + 1, dtype=jnp.int32)
    return counts.at[0].set(BLOCK_ROWS)


def block_scale(key, extent, split, smallest, high):
    gain, own = 1.0, jax.random.fold_in(key, 6)
    for axis_at, blocks in split:
        draws = jnp.exp(jax.random.uniform(jax.random.fold_in(own, axis_at), (blocks,), jnp.float32, smallest / len(split), high / len(split)))
        gain = gain * jnp.repeat(draws, extent[axis_at] // blocks).reshape([-1 if axis == axis_at else 1 for axis in range(len(extent))])
    return gain


def normal_values(own_key, shape, deviation, reach, shards=(), kind=jnp.bfloat16):
    level = block_scale(own_key, shape, shards, -0.22, 0.18) if shards else 1.0
    entries = jax.random.normal(own_key, shape, jnp.float32) * deviation * level
    return jnp.minimum(jnp.maximum(entries, -reach), reach).astype(kind)


def setup_inputs(seed: int = 0, part: int = 0) -> dict:
    streams_of = jax.random.split(jax.random.key(seed), 12)
    part_splits = jax.random.split(jax.random.fold_in(streams_of[11], part), 12)
    return {
        "hidden_norm_rows": normal_values(part_splits[0], (ROWS, MODEL_WIDTH), 1.0, 6.0, ((0, 16),)),
        "value_weight": normal_values(streams_of[1], (MODEL_WIDTH, KEY_VALUE_WIDTH), MODEL_WIDTH ** -0.5, 0.0625, ((0, 16),)),
        "adapter_down_weight": normal_values(streams_of[2], (ADAPTER_TOTAL, MODEL_WIDTH, ADAPTER_RANK), MODEL_WIDTH ** -0.5, 0.0625, ((0, 16),)),
        "adapter_up_weight": normal_values(streams_of[3], (ADAPTER_TOTAL, ADAPTER_RANK, KEY_VALUE_WIDTH), ADAPTER_RANK ** -0.5, 0.75, ((0, 16),)),
        "adapter_per_block": jax.random.randint(part_splits[4], (BLOCKS,), 0, ADAPTER_TOTAL).astype(jnp.int32),
        "block_live_rows": draw_block_live_rows(jax.random.fold_in(jax.random.fold_in(streams_of[11], part), 71), part),
        "queries": draw_queries(jax.random.fold_in(jax.random.fold_in(streams_of[11], part), 71), part),
        "incoming_key": normal_values(part_splits[7], (ROWS, KEY_VALUE_WIDTH), 1.0, 6.0, ((0, 16),)),
        "key_cache": draw_key_cache(jax.random.fold_in(jax.random.fold_in(streams_of[11], part), 71), part),
        "value_cache": normal_values(part_splits[9], (ROWS, CACHE, KEY_VALUE_WIDTH), 1.0, 6.0, ((0, 16),)),
        "cache_length": draw_cache_length(jax.random.fold_in(jax.random.fold_in(streams_of[11], part), 71), part),
    }


def reference(hidden_norm_rows, value_weight, adapter_down_weight, adapter_up_weight, adapter_per_block, block_live_rows, queries, incoming_key, key_cache, value_cache, cache_length):
    group = HEADS // KV_HEADS
    scale = HD ** -0.5
    row_ids = jnp.arange(ROWS, dtype=jnp.int32)
    block_of = row_ids // BLOCK_ROWS
    live = ((row_ids % BLOCK_ROWS) < block_live_rows[block_of]).astype(jnp.float32)[:, None]
    base = jnp.dot(hidden_norm_rows, value_weight, preferred_element_type=jnp.float32)
    selected_down = adapter_down_weight[adapter_per_block].astype(jnp.float32)
    selected_up = adapter_up_weight[adapter_per_block].astype(jnp.float32)
    grouped_by_block = hidden_norm_rows.reshape(BLOCKS, BLOCK_ROWS, MODEL_WIDTH).astype(jnp.float32)
    reduced_rank_state = jnp.einsum("azy,ayu->azu", grouped_by_block, selected_down).astype(jnp.bfloat16)
    delta = jnp.einsum("bkr,brc->bkc", reduced_rank_state.astype(jnp.float32), selected_up).reshape(ROWS, KEY_VALUE_WIDTH)
    new_value = (live * (base + delta)).astype(jnp.bfloat16)
    query = queries.reshape(ROWS, KV_HEADS, group, HD).astype(jnp.float32)
    keys = key_cache.reshape(ROWS, CACHE, KV_HEADS, HD).astype(jnp.float32)
    scores = jnp.einsum("rgqd,rpgd->rgqp", query, keys) * scale
    valid = jnp.arange(CACHE, dtype=jnp.int32)[None, :] < cache_length[:, None]
    scores = jnp.where(valid[:, None, None, :], scores, -1e30)
    fresh = incoming_key.reshape(ROWS, KV_HEADS, HD).astype(jnp.float32)
    score_new = jnp.einsum("rgqd,rgd->rgq", query, fresh) * scale
    top = jnp.maximum(jnp.max(scores, axis=-1), score_new)
    expo = jnp.exp(scores - top[..., None])
    expo_new = jnp.exp(score_new - top)
    total = jnp.sum(expo, axis=-1) + expo_new
    weights = lax.optimization_barrier((expo / total[..., None]).astype(jnp.bfloat16))
    weight_new = lax.optimization_barrier((expo_new / total).astype(jnp.bfloat16))
    values = value_cache.reshape(ROWS, CACHE, KV_HEADS, HD).astype(jnp.float32)
    mixed = jnp.einsum("rgqp,rpgd->rgqd", weights.astype(jnp.float32), values)
    own_value = new_value.reshape(ROWS, KV_HEADS, 1, HD).astype(jnp.float32)
    mixed = mixed + weight_new.astype(jnp.float32)[..., None] * own_value
    attended = (live * mixed.reshape(ROWS, HEADS * HD)).astype(jnp.bfloat16)
    return new_value, attended
```

```python
import functools

import jax
import jax.numpy as jnp
from jax import lax
from jax.experimental import pallas as pl
from jax.experimental.pallas import tpu as pltpu
from jax.sharding import PartitionSpec as P

HEADS = 64
KV_HEADS = 8
HD = 128
BLOCK_ROWS = 128
GROUP = HEADS // KV_HEADS
PLANE = 4
NT = (((1,), (1,)), ((), ()))


def kernel(
    n,
    adapter_ref,
    live_ref,
    length_ref,
    hidden_ref,
    weight_hbm,
    down_hbm,
    up_hbm,
    query_hbm,
    fresh_hbm,
    key_hbm,
    value_hbm,
    new_value_ref,
    attended_ref,
    gathered,
    plane_rows,
    partial,
    landed,
    weight_v,
    down_v,
    up_v,
    query_v,
    fresh_v,
    key_v,
    value_v,
    mix_v,
    fresh_weight_v,
    local_sem,
    send_sem,
    recv_sem,
    sum_send_sem,
    sum_recv_sem,
):
    rows = hidden_ref.shape[0]
    features = weight_v.shape[0]
    resident = down_v.shape[0]
    cached = key_v.shape[1]
    planes = n // PLANE
    me = lax.axis_index("adapt")
    core = lax.rem(me, 2)
    column = lax.rem(lax.div(me, 2), 2)
    level = lax.div(me, PLANE)

    def at(z, y, c):
        return z * PLANE + y * 2 + c

    locals_ = [
        pltpu.make_async_copy(src, dst, local_sem.at[i])
        for i, (src, dst) in enumerate(
            [
                (query_hbm, query_v),
                (fresh_hbm, fresh_v),
                (key_hbm, key_v),
                (value_hbm, value_v),
                (hidden_ref, gathered.at[me]),
                (weight_hbm, weight_v),
                (up_hbm, up_v),
                (down_hbm, down_v),
            ]
        )
    ]
    for copy in locals_:
        copy.start()

    barrier = pltpu.get_barrier_semaphore()
    for k in range(1, n):
        pl.semaphore_signal(
            barrier,
            inc=1,
            device_id={"adapt": lax.rem(me + k, n)},
            device_id_type=pl.DeviceIdType.MESH,
        )
    pl.semaphore_wait(barrier, n - 1)

    sends = []

    def give(block, target, own=False):
        copy = pltpu.make_async_remote_copy(
            src_ref=hidden_ref if own else gathered.at[block],
            dst_ref=gathered.at[block],
            send_sem=send_sem.at[len(sends)],
            recv_sem=recv_sem.at[block],
            device_id={"adapt": target},
            device_id_type=pl.DeviceIdType.MESH,
        )
        copy.start()
        sends.append(copy)

    def take(block):
        pltpu.make_async_remote_copy(
            src_ref=gathered.at[block],
            dst_ref=gathered.at[block],
            send_sem=send_sem.at[0],
            recv_sem=recv_sem.at[block],
            device_id={"adapt": at(level, column, 1 - core)},
            device_id_type=pl.DeviceIdType.MESH,
        ).wait_recv()

    sibling = at(level, column, 1 - core)
    across = at(level, 1 - column, core)
    give(me, across, own=True)
    for k in range(1, planes):
        give(me, at(lax.rem(level + k, planes), column, core), own=True)
    give(me, sibling, own=True)

    sequence = lax.broadcasted_iota(jnp.int32, (rows * GROUP, 1), 0)
    row_of = lax.rem(sequence, rows)
    lengths = jnp.zeros((rows * GROUP, 1), jnp.int32)
    for r in range(rows):
        lengths = jnp.where(row_of == r, length_ref[r], lengths)
    position = lax.broadcasted_iota(jnp.int32, (rows * GROUP, rows * cached), 1)
    valid = (lax.div(position, cached) == row_of) & (lax.rem(position, cached) < lengths)
    scale = HD ** (-0.5)

    def attend(g):
        q = jnp.concatenate(
            [
                query_v[:, (g * GROUP + h) * HD : (g * GROUP + h + 1) * HD].astype(jnp.float32)
                for h in range(GROUP)
            ],
            axis=0,
        )
        keys = key_v[:, :, g * HD : (g + 1) * HD].reshape(rows * cached, HD)
        values = value_v[:, :, g * HD : (g + 1) * HD].reshape(rows * cached, HD)
        fresh = jnp.concatenate(
            [fresh_v[:, g * HD : (g + 1) * HD].astype(jnp.float32)] * GROUP, axis=0
        )
        scores = (
            lax.dot_general(q.astype(jnp.bfloat16), keys, NT, preferred_element_type=jnp.float32)
            * scale
        )
        scores = jnp.where(valid, scores, -1e30)
        score_new = jnp.sum(q * fresh, axis=1, keepdims=True) * scale
        top = jnp.maximum(jnp.max(scores, axis=1, keepdims=True), score_new)
        expo = jnp.exp(scores - top)
        expo_new = jnp.exp(score_new - top)
        inverse = 1.0 / (jnp.sum(expo, axis=1, keepdims=True) + expo_new)
        weights = (expo * inverse).astype(jnp.bfloat16)
        mix_v[g] = jnp.dot(weights, values, preferred_element_type=jnp.float32)
        fresh_weight_v[g] = jnp.broadcast_to(
            (expo_new * inverse).astype(jnp.bfloat16).astype(jnp.float32), (rows * GROUP, HD)
        )

    sum_sends = []

    def process(k):
        z = lax.rem(level + planes - k, planes)
        for y, c in ((column, 1 - core), (1 - column, 1 - core)):
            take(at(z, y, c))
        plane_rows[...] = jnp.concatenate(
            [gathered[z * PLANE + i].astype(jnp.float32) for i in range(PLANE)], axis=0
        ).astype(jnp.bfloat16)
        wanted = adapter_ref[lax.div(z * PLANE * rows, BLOCK_ROWS)] - me * resident
        held = (wanted >= 0) & (wanted < resident)
        wanted = jnp.clip(wanted, 0, resident - 1)
        state = lax.dot_general(
            plane_rows[...], down_v[wanted], NT, preferred_element_type=jnp.float32
        )
        columns = pl.ds(pl.multiple_of(me * features, features), features)
        base = jnp.dot(
            plane_rows[:, columns], weight_v[...], preferred_element_type=jnp.float32
        )
        delta = jnp.dot(
            state.astype(jnp.bfloat16), up_v[wanted], preferred_element_type=jnp.float32
        )
        share = base + jnp.where(held, delta, 0.0)
        for i in range(PLANE):
            partial[z * PLANE + i] = share[i * rows : (i + 1) * rows].astype(jnp.bfloat16)
        targets = [at(z, y, c) for y in (1 - column, column) for c in (core, 1 - core)]
        if k == 0:
            targets = [at(z, 1 - column, core), at(z, 1 - column, 1 - core), sibling]
        for target in targets:
            copy = pltpu.make_async_remote_copy(
                src_ref=partial.at[target],
                dst_ref=landed.at[me],
                send_sem=sum_send_sem.at[len(sum_sends)],
                recv_sem=sum_recv_sem.at[me],
                device_id={"adapt": target},
                device_id_type=pl.DeviceIdType.MESH,
            )
            copy.start()
            sum_sends.append(copy)

    for copy in locals_[:4]:
        copy.wait()
    attend(0)
    attend(1)
    take(across)
    give(across, sibling)
    attend(2)
    attend(3)
    for copy in locals_[4:]:
        copy.wait()
    todo = list(range(4, KV_HEADS))
    for k in range(1, planes):
        z = lax.rem(level + planes - k, planes)
        block = at(z, column, core)
        take(block)
        give(block, across)
        give(block, sibling)
        if k >= 2:
            before = at(lax.rem(level + planes - (k - 1), planes), 1 - column, core)
            take(before)
            give(before, sibling)
        process(k - 1)
        if todo:
            attend(todo.pop(0))
    last = at(lax.rem(level + 1, planes), 1 - column, core)
    if planes > 1:
        take(last)
        give(last, sibling)
    while todo:
        attend(todo.pop(0))
    process(planes - 1)

    total = partial[me].astype(jnp.float32)
    for k in range(1, n):
        source = lax.rem(me + k, n)
        pltpu.make_async_remote_copy(
            src_ref=partial.at[source],
            dst_ref=landed.at[source],
            send_sem=sum_send_sem.at[0],
            recv_sem=sum_recv_sem.at[source],
            device_id={"adapt": source},
            device_id_type=pl.DeviceIdType.MESH,
        ).wait_recv()
        total = total + landed[source].astype(jnp.float32)
    first = me * rows
    local = lax.rem(first, BLOCK_ROWS) + lax.broadcasted_iota(jnp.int32, (rows, 1), 0)
    live = (local < live_ref[lax.div(first, BLOCK_ROWS)]).astype(jnp.float32)
    new_value = (live * total).astype(jnp.bfloat16)
    new_value_ref[...] = new_value
    own = new_value.astype(jnp.float32)
    for g in range(KV_HEADS):
        own_group = own[:, g * HD : (g + 1) * HD]
        for h in range(GROUP):
            part = slice(h * rows, (h + 1) * rows)
            mixed = mix_v[g, part, :] + fresh_weight_v[g, part, :] * own_group
            head = g * GROUP + h
            attended_ref[:, head * HD : (head + 1) * HD] = (live * mixed).astype(jnp.bfloat16)
    for copy in sends + sum_sends:
        copy.wait_send()


def on_device(
    n,
    hidden_norm_rows,
    value_weight,
    adapter_down_weight,
    adapter_up_weight,
    adapter_per_block,
    block_live_rows,
    queries,
    incoming_key,
    key_cache,
    value_cache,
    cache_length,
):
    rows, width = hidden_norm_rows.shape
    down = jnp.swapaxes(adapter_down_weight, 1, 2)
    wide = value_weight.shape[1]
    planes = n // PLANE
    bf16 = jnp.bfloat16
    sends = 3 * (planes - 1) + 2 + planes
    smem = pl.BlockSpec(memory_space=pltpu.SMEM)
    anywhere = pl.BlockSpec(memory_space=pl.ANY)
    vmem = pl.BlockSpec(memory_space=pltpu.VMEM)
    return pl.pallas_call(
        functools.partial(kernel, n),
        out_shape=(
            jax.ShapeDtypeStruct((rows, wide), bf16),
            jax.ShapeDtypeStruct(queries.shape, bf16),
        ),
        in_specs=[smem] * 3 + [anywhere] * 8,
        out_specs=(vmem, vmem),
        scratch_shapes=[
            pltpu.VMEM((n, rows, width), bf16),
            pltpu.VMEM((PLANE * rows, width), bf16),
            pltpu.VMEM((n, rows, wide), bf16),
            pltpu.VMEM((n, rows, wide), bf16),
            pltpu.VMEM(value_weight.shape, bf16),
            pltpu.VMEM(down.shape, bf16),
            pltpu.VMEM(adapter_up_weight.shape, bf16),
            pltpu.VMEM(queries.shape, bf16),
            pltpu.VMEM(incoming_key.shape, bf16),
            pltpu.VMEM(key_cache.shape, bf16),
            pltpu.VMEM(value_cache.shape, bf16),
            pltpu.VMEM((KV_HEADS, GROUP * rows, HD), jnp.float32),
            pltpu.VMEM((KV_HEADS, GROUP * rows, HD), jnp.float32),
            pltpu.SemaphoreType.DMA((8,)),
            pltpu.SemaphoreType.DMA((sends,)),
            pltpu.SemaphoreType.DMA((n,)),
            pltpu.SemaphoreType.DMA((n,)),
            pltpu.SemaphoreType.DMA((n,)),
        ],
        compiler_params=pltpu.CompilerParams(
            collective_id=0, has_side_effects=True, vmem_limit_bytes=48 * 1024 * 1024
        ),
    )(
        adapter_per_block,
        block_live_rows,
        cache_length,
        hidden_norm_rows,
        value_weight,
        down,
        adapter_up_weight,
        queries,
        incoming_key,
        key_cache,
        value_cache,
    )


def solution(mesh):
    return jax.shard_map(
        functools.partial(on_device, mesh.shape["adapt"]),
        mesh=mesh,
        in_specs=(
            P(("parts", "adapt"), None),
            P("adapt", None),
            P("adapt", None, None),
            P("adapt", None, None),
            P("parts"),
            P("parts"),
            P(("parts", "adapt"), None),
            P(("parts", "adapt"), None),
            P(("parts", "adapt"), None, None),
            P(("parts", "adapt"), None, None),
            P(("parts", "adapt")),
        ),
        out_specs=(P(("parts", "adapt"), None), P(("parts", "adapt"), None)),
        check_vma=False,
    )
```

```python
import functools

import jax
import jax.numpy as jnp
from jax import lax
from jax.experimental import pallas as pl
from jax.experimental.pallas import tpu as pltpu
from jax.sharding import PartitionSpec as P

HEADS = 64
KV_HEADS = 8
HD = 128
BLOCK_ROWS = 128
GROUP = HEADS // KV_HEADS
PLANE = 4
NT = (((1,), (1,)), ((), ()))


def kernel(
    n,
    adapter_ref,
    live_ref,
    length_ref,
    hidden_hbm,
    weight_hbm,
    down_hbm,
    up_hbm,
    query_hbm,
    fresh_hbm,
    key_hbm,
    value_hbm,
    new_value_ref,
    attended_ref,
    hidden_v,
    quarters,
    gathered,
    plane_rows,
    partial,
    landed,
    weight_v,
    down_v,
    up_v,
    down_own,
    down_chip,
    down_plane,
    up_own,
    up_chip,
    up_plane,
    query_v,
    fresh_v,
    key_v,
    value_v,
    mix_v,
    fresh_weight_v,
    local_sem,
    send_sem,
    mate_sem,
    gather_sem,
    pair_sem,
    sum_send_sem,
    sum_recv_sem,
):
    rows = hidden_v.shape[0]
    features = weight_v.shape[0]
    resident = down_v.shape[0]
    cached = key_v.shape[1]
    blocks = down_own.shape[1]
    half = up_own.shape[3]
    planes = n // PLANE
    me = lax.axis_index("adapt")
    core = lax.rem(me, 2)
    column = lax.rem(lax.div(me, 2), 2)
    level = lax.div(me, PLANE)
    mine = column * 2 + core
    f32, bf16 = jnp.float32, jnp.bfloat16

    def at(z, q):
        return z * PLANE + q

    locals_ = [
        pltpu.make_async_copy(src, dst, local_sem.at[i])
        for i, (src, dst) in enumerate(
            [
                (hidden_hbm, hidden_v),
                (down_hbm, down_v),
                (up_hbm, up_v),
                (query_hbm, query_v),
                (fresh_hbm, fresh_v),
                (key_hbm, key_v),
                (value_hbm, value_v),
                (weight_hbm, weight_v),
            ]
        )
    ]
    for copy in locals_:
        copy.start()

    barrier = pltpu.get_barrier_semaphore()
    for k in range(1, n):
        pl.semaphore_signal(
            barrier,
            inc=1,
            device_id={"adapt": lax.rem(me + k, n)},
            device_id_type=pl.DeviceIdType.MESH,
        )

    locals_[0].wait()
    for q in range(PLANE):
        for z in range(planes):
            first = (z * PLANE + q) * features
            quarters[q, :, z * features : (z + 1) * features] = hidden_v[
                :, first : first + features
            ]
    gathered[level, mine] = quarters[mine]
    pl.semaphore_wait(barrier, n - 1)

    sends = []

    def remote(src, dst, recv, target):
        return pltpu.make_async_remote_copy(
            src_ref=src,
            dst_ref=dst,
            send_sem=send_sem.at[min(len(sends), send_sem.shape[0] - 1)],
            recv_sem=recv,
            device_id={"adapt": target},
            device_id_type=pl.DeviceIdType.MESH,
        )

    def give(src, dst, recv, target):
        copy = remote(src, dst, recv, target)
        copy.start()
        sends.append(copy)

    sibling_place = column * 2 + 1 - core
    across_place = (1 - column) * 2 + core
    corner_place = (1 - column) * 2 + 1 - core
    mates = (across_place, corner_place, sibling_place)
    sibling, across = at(level, sibling_place), at(level, across_place)
    for q in mates:
        give(quarters.at[q], gathered.at[level, mine], mate_sem.at[mine], at(level, q))

    def take(ref, recv):
        remote(ref, ref, recv, sibling).wait_recv()

    locals_[1].wait()
    locals_[2].wait()
    for b in range(blocks):
        wanted = adapter_ref[b] - me * resident
        held = (wanted >= 0) & (wanted < resident)
        wanted = jnp.clip(wanted, 0, resident - 1)
        keep = jnp.where(held, 1.0, 0.0).astype(bf16)
        for q in range(PLANE):
            for z in range(planes):
                first = (z * PLANE + q) * features
                down_own[q, b, :, z * features : (z + 1) * features] = (
                    down_v[wanted, :, first : first + features] * keep
                )
        for c in range(2):
            up_own[c, b] = up_v[wanted, :, c * half : (c + 1) * half] * keep
    give(down_own.at[corner_place], down_chip.at[1 - column], pair_sem.at[0], sibling)
    give(down_own.at[sibling_place], down_chip.at[column], pair_sem.at[1], sibling)
    give(up_own, up_chip, pair_sem.at[2], sibling)

    for q in mates:
        take(gathered.at[level, q], mate_sem.at[q])
    for k in range(1, planes):
        give(
            gathered.at[level],
            gathered.at[level],
            gather_sem.at[level],
            at(lax.rem(level + k, planes), mine),
        )

    take(down_chip.at[1 - column], pair_sem.at[0])
    down_own[across_place] = down_own[across_place] + down_chip[1 - column]
    give(down_own.at[across_place], down_plane, pair_sem.at[3], across)
    take(up_chip, pair_sem.at[2])
    for c in range(2):
        up_chip[c] = up_chip[c] + up_own[c]
    give(up_chip.at[core], up_plane.at[core], pair_sem.at[4], across)
    up_sent = sends[-1]

    sequence = lax.broadcasted_iota(jnp.int32, (rows * GROUP, 1), 0)
    row_of = lax.rem(sequence, rows)
    lengths = jnp.zeros((rows * GROUP, 1), jnp.int32)
    for r in range(rows):
        lengths = jnp.where(row_of == r, length_ref[r], lengths)
    position = lax.broadcasted_iota(jnp.int32, (rows * GROUP, rows * cached), 1)
    valid = (lax.div(position, cached) == row_of) & (lax.rem(position, cached) < lengths)
    scale = HD ** (-0.5)

    def attend(g):
        q = jnp.concatenate(
            [
                query_v[:, (g * GROUP + h) * HD : (g * GROUP + h + 1) * HD].astype(jnp.float32)
                for h in range(GROUP)
            ],
            axis=0,
        )
        keys = key_v[:, :, g * HD : (g + 1) * HD].reshape(rows * cached, HD)
        values = value_v[:, :, g * HD : (g + 1) * HD].reshape(rows * cached, HD)
        fresh = jnp.concatenate(
            [fresh_v[:, g * HD : (g + 1) * HD].astype(jnp.float32)] * GROUP, axis=0
        )
        scores = (
            lax.dot_general(q.astype(jnp.bfloat16), keys, NT, preferred_element_type=jnp.float32)
            * scale
        )
        scores = jnp.where(valid, scores, -1e30)
        score_new = jnp.sum(q * fresh, axis=1, keepdims=True) * scale
        top = jnp.maximum(jnp.max(scores, axis=1, keepdims=True), score_new)
        expo = jnp.exp(scores - top)
        expo_new = jnp.exp(score_new - top)
        inverse = 1.0 / (jnp.sum(expo, axis=1, keepdims=True) + expo_new)
        weights = (expo * inverse).astype(jnp.bfloat16)
        mix_v[g] = jnp.dot(weights, values, preferred_element_type=jnp.float32)
        fresh_weight_v[g] = jnp.broadcast_to(
            (expo_new * inverse).astype(jnp.bfloat16).astype(jnp.float32), (rows * GROUP, HD)
        )

    sum_sends = []

    def process(k):
        z = lax.rem(level + planes - k, planes)
        if k:
            take(gathered.at[z], gather_sem.at[z])
        plane_rows[...] = jnp.concatenate(
            [gathered[z, q].astype(f32) for q in range(PLANE)], axis=0
        ).astype(bf16)
        block = lax.div(z * PLANE * rows, BLOCK_ROWS)
        state = lax.dot_general(
            plane_rows[...], down_own[mine, block], NT, preferred_element_type=f32
        ).astype(bf16)
        columns = pl.ds(pl.multiple_of(level * features, features), features)
        base = jnp.dot(plane_rows[:, columns], weight_v[...], preferred_element_type=f32)
        for c in range(2):
            lanes = slice(c * half, (c + 1) * half)
            share = base[:, lanes] + jnp.dot(
                state, up_chip[c, block], preferred_element_type=f32
            )
            for q in range(PLANE):
                partial[z * PLANE + q, :, lanes] = share[q * rows : (q + 1) * rows].astype(bf16)
        for q in mates if k == 0 else mates + (mine,):
            target = at(z, q)
            copy = pltpu.make_async_remote_copy(
                src_ref=partial.at[target],
                dst_ref=landed.at[me],
                send_sem=sum_send_sem.at[len(sum_sends)],
                recv_sem=sum_recv_sem.at[me],
                device_id={"adapt": target},
                device_id_type=pl.DeviceIdType.MESH,
            )
            copy.start()
            sum_sends.append(copy)

    for copy in locals_[3:]:
        copy.wait()
    for g in range(KV_HEADS // 2):
        attend(g)
    take(up_plane.at[core], pair_sem.at[4])
    give(up_plane.at[core], up_plane.at[core], pair_sem.at[5], sibling)
    for g in range(KV_HEADS // 2, KV_HEADS):
        attend(g)
    take(down_chip.at[column], pair_sem.at[1])
    take(down_plane, pair_sem.at[3])
    down_own[mine] = down_own[mine] + down_chip[column] + down_plane[...]
    take(up_plane.at[1 - core], pair_sem.at[5])
    up_sent.wait_send()
    for c in range(2):
        up_chip[c] = up_chip[c] + up_plane[c]
    for k in range(planes):
        process(k)

    total = partial[me].astype(jnp.float32)
    for k in range(1, n):
        source = lax.rem(me + k, n)
        pltpu.make_async_remote_copy(
            src_ref=partial.at[source],
            dst_ref=landed.at[source],
            send_sem=sum_send_sem.at[0],
            recv_sem=sum_recv_sem.at[source],
            device_id={"adapt": source},
            device_id_type=pl.DeviceIdType.MESH,
        ).wait_recv()
        total = total + landed[source].astype(jnp.float32)
    first = me * rows
    local = lax.rem(first, BLOCK_ROWS) + lax.broadcasted_iota(jnp.int32, (rows, 1), 0)
    live = (local < live_ref[lax.div(first, BLOCK_ROWS)]).astype(jnp.float32)
    new_value = (live * total).astype(jnp.bfloat16)
    new_value_ref[...] = new_value
    own = new_value.astype(jnp.float32)
    for g in range(KV_HEADS):
        own_group = own[:, g * HD : (g + 1) * HD]
        for h in range(GROUP):
            part = slice(h * rows, (h + 1) * rows)
            mixed = mix_v[g, part, :] + fresh_weight_v[g, part, :] * own_group
            head = g * GROUP + h
            attended_ref[:, head * HD : (head + 1) * HD] = (live * mixed).astype(jnp.bfloat16)
    for copy in sends + sum_sends:
        if copy is not up_sent:
            copy.wait_send()


def on_device(
    n,
    hidden_norm_rows,
    value_weight,
    adapter_down_weight,
    adapter_up_weight,
    adapter_per_block,
    block_live_rows,
    queries,
    incoming_key,
    key_cache,
    value_cache,
    cache_length,
):
    rows, width = hidden_norm_rows.shape
    down = jnp.swapaxes(adapter_down_weight, 1, 2)
    wide = value_weight.shape[1]
    planes = n // PLANE
    bf16 = jnp.bfloat16
    blocks = adapter_per_block.shape[0]
    sends = 3 + 3 + (planes - 1) + 2 + 1
    rank, quarter, half = down.shape[1], width // PLANE, wide // 2
    smem = pl.BlockSpec(memory_space=pltpu.SMEM)
    anywhere = pl.BlockSpec(memory_space=pl.ANY)
    vmem = pl.BlockSpec(memory_space=pltpu.VMEM)
    return pl.pallas_call(
        functools.partial(kernel, n),
        out_shape=(
            jax.ShapeDtypeStruct((rows, wide), bf16),
            jax.ShapeDtypeStruct(queries.shape, bf16),
        ),
        in_specs=[smem] * 3 + [anywhere] * 8,
        out_specs=(vmem, vmem),
        scratch_shapes=[
            pltpu.VMEM((rows, width), bf16),
            pltpu.VMEM((PLANE, rows, quarter), bf16),
            pltpu.VMEM((planes, PLANE, rows, quarter), bf16),
            pltpu.VMEM((PLANE * rows, quarter), bf16),
            pltpu.VMEM((n, rows, wide), bf16),
            pltpu.VMEM((n, rows, wide), bf16),
            pltpu.VMEM(value_weight.shape, bf16),
            pltpu.VMEM(down.shape, bf16),
            pltpu.VMEM(adapter_up_weight.shape, bf16),
            pltpu.VMEM((PLANE, blocks, rank, quarter), bf16),
            pltpu.VMEM((2, blocks, rank, quarter), bf16),
            pltpu.VMEM((blocks, rank, quarter), bf16),
            pltpu.VMEM((2, blocks, rank, half), bf16),
            pltpu.VMEM((2, blocks, rank, half), bf16),
            pltpu.VMEM((2, blocks, rank, half), bf16),
            pltpu.VMEM(queries.shape, bf16),
            pltpu.VMEM(incoming_key.shape, bf16),
            pltpu.VMEM(key_cache.shape, bf16),
            pltpu.VMEM(value_cache.shape, bf16),
            pltpu.VMEM((KV_HEADS, GROUP * rows, HD), jnp.float32),
            pltpu.VMEM((KV_HEADS, GROUP * rows, HD), jnp.float32),
            pltpu.SemaphoreType.DMA((8,)),
            pltpu.SemaphoreType.DMA((sends,)),
            pltpu.SemaphoreType.DMA((PLANE,)),
            pltpu.SemaphoreType.DMA((planes,)),
            pltpu.SemaphoreType.DMA((6,)),
            pltpu.SemaphoreType.DMA((n,)),
            pltpu.SemaphoreType.DMA((n,)),
        ],
        compiler_params=pltpu.CompilerParams(
            collective_id=0, has_side_effects=True, vmem_limit_bytes=63 * 1024 * 1024
        ),
    )(
        adapter_per_block,
        block_live_rows,
        cache_length,
        hidden_norm_rows,
        value_weight,
        down,
        adapter_up_weight,
        queries,
        incoming_key,
        key_cache,
        value_cache,
    )


def solution(mesh):
    return jax.shard_map(
        functools.partial(on_device, mesh.shape["adapt"]),
        mesh=mesh,
        in_specs=(
            P(("parts", "adapt"), None),
            P("adapt", None),
            P("adapt", None, None),
            P("adapt", None, None),
            P("parts"),
            P("parts"),
            P(("parts", "adapt"), None),
            P(("parts", "adapt"), None),
            P(("parts", "adapt"), None, None),
            P(("parts", "adapt"), None, None),
            P(("parts", "adapt")),
        ),
        out_specs=(P(("parts", "adapt"), None), P(("parts", "adapt"), None)),
        check_vma=False,
    )
```
